1024 devices in a mesh: dp: 128 (over y_lo, z, core), tensor: 8 (over y_hi, x).
Axes of the slice: x: 4, y: 8 (y_hi: 2, y_lo: 4; y = y_hi * 4 + y_lo), z: 16, core: 2. Of those that a mesh axis runs over, the one named last changes fastest.
Arguments:
- out_grad: bfloat16 [131072, 2560], P(('dp', 'tensor')), may hold values from -24 to 24
- context: bfloat16 [131072, 2560], P('dp', 'tensor'), may hold values from -0.015625 to 0.015625
- out_weight: bfloat16 [2560, 2560], P(None, 'tensor'), may hold values from -0.125 to 0.125
- dropout_seeds: int32 [128, 1], P('dp'), may hold values from 0 to 16777215
Outputs:
- grad_context: bfloat16 [131072, 2560], P('dp', 'tensor')
- grad_out_weight: float32 [2560, 2560], P('dp', 'tensor')
The draws below stay inside these ranges and needn't reach their ends.
All inputs are finite; a program needn't handle non-finite values.
Results may differ from the reference program's by a relative error of at most 0.0049.
Values may be sent and summed in bfloat16 or wider, within the bound.
A program may use at most 64 MiB of HBM per device.

```python
import jax
import jax.numpy as jnp
from jax import lax

DW = 2560
HQ = 2560
BATCH = 128
TOKENS = 131072


def with_ends(values, stream_key, smallest, largest):
    index_at = [jax.random.randint(jax.random.fold_in(stream_key, axis), (), 0, length) for axis, length in enumerate(values.shape)]
    widest = values.shape.index(max(values.shape))
    next_to = index_at[:widest] + [(index_at[widest] + 1) % values.shape[widest]] + index_at[widest + 1:]
    return values.at[tuple(index_at)].set(smallest).at[tuple(next_to)].set(largest)


def spiked(result, rng, source, target, shards_of, factor):
    owner, partner = [(jnp.arange(result.shape[dim]) // (result.shape[dim] // shards_of)).reshape([-1 if axis == dim else 1 for axis in range(result.ndim)]) for dim in (source, target)]
    chosen = jax.random.permutation(rng, shards_of)[partner]
    strong = (owner == chosen) | (owner == (partner + shards_of // 2) % shards_of)
    return jnp.where(strong, factor * result, result)


def steps_of(own_key, shape, shards, low, top_value):
    gain = 1.0
    for dim, shards_of in shards:
        heights = jax.random.uniform(jax.random.fold_in(jax.random.fold_in(own_key, 6), dim), (shards_of,), jnp.float32, low / len(shards), top_value / len(shards))
        gain = gain * jnp.repeat(jnp.exp(heights), shape[dim] // shards_of).reshape((-1,) + (1,) * (len(shape) - 1 - dim))
    return gain


def gaussian(key, shape, deviation, limit, pieces=(), held_as=jnp.bfloat16):
    array = deviation * jax.random.normal(key, shape, jnp.float32)
    if pieces:
        array = array * steps_of(key, shape, pieces, -0.22, 0.18)
    return jnp.clip(array, -limit, limit).astype(held_as)


def noise_with(own_key, extent, deviation, limit, cuts, heavy, held_as=jnp.bfloat16):
    result = deviation * jax.random.normal(own_key, extent, jnp.float32)
    if cuts:
        result = result * steps_of(own_key, extent, cuts, -0.22, 0.18)
    return jnp.clip(spiked(result, jax.random.fold_in(own_key, 3), *heavy), -limit, limit).astype(held_as)


def setup_inputs(seed: int = 0) -> dict:
    key_list = jax.random.split(jax.random.key(seed), 5)
    return {
        "out_grad": noise_with(key_list[0], (TOKENS, DW), 1.0, 24.0, ((0, 1024),), (0, 1, 512, 6.0)),
        "context": gaussian(key_list[1], (TOKENS, HQ), TOKENS ** -0.5, 0.015625, ((0, 128), (1, 8))),
        "out_weight": gaussian(key_list[2], (DW, HQ), DW ** -0.5, 0.125, ((1, 8),)),
        "dropout_seeds": with_ends(jax.random.randint(key_list[3], (BATCH, 1), 0, 16777216), jax.random.fold_in(key_list[3], 1), 0, 16777215).astype(jnp.int32),
    }


KEEP_SCALE = 1.0 / 0.9


def keep_bits(seed_word, position):
    hashed = position * jnp.int32(-1640531535) + seed_word
    hashed = hashed ^ lax.shift_right_logical(hashed, jnp.int32(15))
    hashed = hashed * jnp.int32(-2048144789)
    hashed = hashed ^ lax.shift_right_logical(hashed, jnp.int32(13))
    hashed = hashed * jnp.int32(-1028477387)
    hashed = hashed ^ lax.shift_right_logical(hashed, jnp.int32(16))
    return (hashed & 1023) >= 102


def reference(out_grad, context, out_weight, dropout_seeds):
    batch_count = dropout_seeds.shape[0]
    seq_len = context.shape[0] // batch_count
    width_out = out_grad.shape[1]
    grads_in = out_grad.reshape(batch_count, seq_len, width_out)
    context_in = context.reshape(batch_count, seq_len, -1)

    def one_sequence(total, inputs):
        grad_rows, context_seq, seed_pair = inputs
        tok_ids = jnp.arange(seq_len, dtype=jnp.int32)[:, None]
        feat_ids = jnp.arange(width_out, dtype=jnp.int32)[None, :]
        branch_keep = keep_bits(seed_pair[0], tok_ids * width_out + feat_ids)
        grad_branch = jnp.where(branch_keep, grad_rows.astype(jnp.float32) * KEEP_SCALE, 0.0).astype(jnp.bfloat16)
        grad_ctx = jnp.dot(grad_branch, out_weight, preferred_element_type=jnp.float32).astype(jnp.bfloat16)
        weight_term = lax.dot_general(grad_branch, context_seq, (((0,), (0,)), ((), ())),
                                      preferred_element_type=jnp.float32)
        return total + weight_term, grad_ctx

    start_total = jnp.zeros((width_out, context.shape[1]), jnp.float32)
    weight_grad, grad_ctx = lax.scan(one_sequence, start_total, (grads_in, context_in, dropout_seeds))
    return grad_ctx.reshape(context.shape), weight_grad
```

```python
import functools

import jax
import jax.numpy as jnp
from jax import lax
from jax.experimental import pallas as pl
from jax.experimental.pallas import tpu as pltpu
from jax.sharding import PartitionSpec as P

KEEP_SCALE = 1.0 / 0.9
NX, NY, NZ = 4, 4, 16
CHUNK = 128
DW, HQ = 2560, 320
PARTS, PART, PER_Z = 5, 512, 32
BLOCK_Y, BLOCK = 640, 40
LANES = 384
FOLD = 80
MESH = pl.DeviceIdType.MESH


def keep_bits(seed_word, position):
    hashed = position * jnp.int32(-1640531535) + seed_word
    hashed = hashed ^ lax.shift_right_logical(hashed, jnp.int32(15))
    hashed = hashed * jnp.int32(-2048144789)
    hashed = hashed ^ lax.shift_right_logical(hashed, jnp.int32(13))
    hashed = hashed * jnp.int32(-1028477387)
    hashed = hashed ^ lax.shift_right_logical(hashed, jnp.int32(16))
    return (hashed & 1023) >= 102


def kernel(
    seed_ref, grad_hbm, ctx_hbm, w_hbm, gc_hbm, gw_ref,
    grad, ctx, w, nat, g, wq, ctxe, acc, wt, own, cs, cr, zs, zr, total, yr, gcb,
    in_sem, out_sem, gsend, grecv, csend, crecv, zsend, zrecv, ysend, yrecv,
):
    d = lax.axis_index("dp")
    t = lax.axis_index("tensor")
    core = lax.rem(d, 2)
    z = lax.rem(d // 2, NZ)
    yl = d // (2 * NZ)
    yh = t // NX
    x = lax.rem(t, NX)
    row = yh * NX
    other = (1 - yh) * NX
    xr, xl, xo = lax.rem(x + 1, NX), lax.rem(x + 3, NX), lax.rem(x + 2, NX)
    right, left, across = {"tensor": row + xr}, {"tensor": row + xl}, {"tensor": other + x}
    sibling = {"dp": d + 1 - 2 * core}
    owner = lax.rem(z, 2) == core

    def at(y_to, z_to, core_to):
        return {"dp": (y_to * NZ + z_to) * 2 + core_to}

    loads = [
        pltpu.make_async_copy(a, b, in_sem.at[i])
        for i, (a, b) in enumerate(((grad_hbm, grad), (w_hbm, w), (ctx_hbm, ctx)))
    ]
    for load in loads:
        load.start()

    barrier = pltpu.get_barrier_semaphore()

    def greet(device):
        pl.semaphore_signal(barrier, inc=1, device_id=device, device_id_type=MESH)

    for device in (across, right, left):
        greet(device)

    def greet_z(i, carry):
        greet(at(yl, lax.rem(z + i, NZ), core))
        return carry

    lax.fori_loop(1, NZ, greet_z, 0)
    for i in range(1, NY):
        for c in range(2):
            greet(at(lax.rem(yl + i, NY), z, c))
    greet(sibling)

    loads[0].wait()
    seed = seed_ref[0, 0]

    def drop(i, carry):
        r = pl.multiple_of(i * 16, 16)
        rows = lax.broadcasted_iota(jnp.int32, (16, DW), 0) + (t * CHUNK + r)
        keep = keep_bits(seed, rows * DW + lax.broadcasted_iota(jnp.int32, (16, DW), 1))
        scaled = grad[pl.ds(r, 16), :].astype(jnp.float32) * KEEP_SCALE
        nat[pl.ds(r, 16), :] = jnp.where(keep, scaled, 0.0).astype(jnp.bfloat16)
        return carry

    lax.fori_loop(0, CHUNK // 16, drop, 0)

    def onehot(q, base, half):
        index = lax.broadcasted_iota(jnp.int32, (256, 1), 0)
        i = PER_Z * q + lax.rem(index, PER_Z)
        y_of = (i >= 40).astype(jnp.int32) + (i >= 80).astype(jnp.int32) + (i >= 120).astype(jnp.int32)
        feature = 600 * y_of + BLOCK * (2 * (index // PER_Z) + half) + i - base
        columns = lax.broadcasted_iota(jnp.int32, (256, 2 * BLOCK_Y), 1)
        return jnp.where(columns == feature, 1.0, 0.0).astype(jnp.bfloat16)

    def base_of(q):
        return pl.multiple_of(jnp.minimum((4 * q) // 5, 2) * BLOCK_Y, BLOCK_Y)

    def prep_grad(q):
        base = base_of(q)

        def body(half, carry):
            p = onehot(q, base, half)
            picked = lax.dot_general(
                nat[:, pl.ds(base, 2 * BLOCK_Y)], p, (((1,), (1,)), ((), ())),
                preferred_element_type=jnp.float32,
            )
            g[q, t, :, pl.ds(pl.multiple_of(half * 256, 256), 256)] = picked.astype(jnp.bfloat16)
            return carry

        lax.fori_loop(0, 2, body, 0)

    def prep_w(q):
        base = base_of(q)

        def body(half, carry):
            p = onehot(q, base, half)
            picked = jnp.dot(p, w[pl.ds(base, 2 * BLOCK_Y), :], preferred_element_type=jnp.float32)
            wq[q, pl.ds(pl.multiple_of(half * 256, 256), 256), :] = picked.astype(jnp.bfloat16)
            return carry

        lax.fori_loop(0, 2, body, 0)

    def piece(q, origin, half):
        if half is None:
            return g.at[q, origin]
        return g.at[q, origin, pl.ds(64 * half, 64)]

    def send(q, origin, half, event, device):
        ref = piece(q, origin, half)
        pltpu.make_async_remote_copy(
            src_ref=ref, dst_ref=ref, send_sem=gsend.at[q, event], recv_sem=grecv.at[q, event],
            device_id=device, device_id_type=MESH,
        ).start()

    def arrived(q, origin, half, event):
        ref = piece(q, origin, half)
        pltpu.make_async_copy(ref, ref, grecv.at[q, event]).wait()

    def send_own(q):
        send(q, t, None, 2, across)
        send(q, t, None, 0, right)
        send(q, t, None, 1, left)

    prep_grad(0)
    pl.semaphore_wait(barrier, 3 + (NZ - 1) + 2 * (NY - 1) + 1)
    send_own(0)
    prep_grad(1)

    loads[1].wait()
    prep_w(0)
    loads[2].wait()
    tail = ctx[:, 256:320]
    ctxe[:, 0:256] = ctx[:, 0:256]
    ctxe[:, 256:384] = jnp.concatenate([tail, tail], axis=1)
    acc[...] = jnp.zeros_like(acc)

    def rows_of(q, start):
        return g[q, pl.ds(start, NX)].reshape(NX * CHUNK, PART)

    def weight_term(q, start):
        tokens = pl.ds(pl.multiple_of(start * CHUNK, NX * CHUNK), NX * CHUNK)
        return lax.dot_general(
            rows_of(q, start), ctxe[tokens, :], (((0,), (0,)), ((), ())),
            preferred_element_type=jnp.float32,
        )

    def context_term(q, start):
        tokens = pl.ds(pl.multiple_of(start * CHUNK, NX * CHUNK), NX * CHUNK)
        acc[tokens, :] += jnp.dot(rows_of(q, start), wq[q], preferred_element_type=jnp.float32)

    low_lanes = lax.broadcasted_iota(jnp.int32, (16, 128), 1) < 64

    def folded(first):
        block = pl.ds(pl.multiple_of(first, PER_Z), PER_Z)
        last = wt[block, 256:384]
        return wt[block, 0:128], wt[block, 128:256], jnp.where(low_lanes, last[0:16], last[16:32])

    def pack(q):
        def body(j, carry):
            a, b, c = folded((1 - core) * 256 + PER_Z * j)
            cs[q, j, 0:32] = a.astype(jnp.bfloat16)
            cs[q, j, 32:64] = b.astype(jnp.bfloat16)
            cs[q, j, 64:80] = c.astype(jnp.bfloat16)
            return carry

        lax.fori_loop(0, NZ // 2, body, 0)
        to_sibling(q).start()

        def mine(j, carry):
            a, b, c = folded(core * 256 + PER_Z * j)
            own[j, 0:32], own[j, 32:64], own[j, 64:80] = a, b, c
            return carry

        lax.fori_loop(0, NZ // 2, mine, 0)

    def to_sibling(q):
        return pltpu.make_async_remote_copy(
            src_ref=cs.at[q], dst_ref=cr.at[q], send_sem=csend.at[q], recv_sem=crecv.at[q],
            device_id=sibling, device_id_type=MESH,
        )

    def z_copy(q, j):
        return pltpu.make_async_remote_copy(
            src_ref=zs.at[q, j], dst_ref=zr.at[q, z], send_sem=zsend.at[q, j], recv_sem=zrecv.at[q],
            device_id=at(yl, 2 * j + core, core), device_id_type=MESH,
        )

    def z_stage(q):
        to_sibling(q).wait_recv()

        def body(j, carry):
            zs[q, j] = (own[j] + cr[q, j].astype(jnp.float32)).astype(jnp.bfloat16)
            return carry

        lax.fori_loop(0, NZ // 2, body, 0)
        for i in (4, 3, 5, 2, 6, 1, 7):
            z_copy(q, lax.rem(z // 2 + i, NZ // 2)).start()

        @pl.when(owner)
        def _():
            pltpu.make_async_copy(zs.at[q, z // 2], zr.at[q, z], zrecv.at[q]).start()

        @pl.when(jnp.logical_not(owner))
        def _():
            z_copy(q, z // 2).start()

    def y_copy(y_to, slot, device):
        return pltpu.make_async_remote_copy(
            src_ref=total.at[pl.ds(pl.multiple_of(BLOCK * y_to, 8), BLOCK)], dst_ref=yr.at[yl],
            send_sem=ysend.at[y_to, slot], recv_sem=yrecv.at[yl],
            device_id=device, device_id_type=MESH,
        )

    def z_sum(q):
        @pl.when(owner)
        def _():
            pltpu.make_async_copy(zr.at[q], zr.at[q], zrecv.at[q]).wait()
            s = zr[q, 0].astype(jnp.float32)
            for i in range(1, NZ):
                s = s + zr[q, i].astype(jnp.float32)
            rows = pl.multiple_of(PER_Z * q, PER_Z)
            total[pl.ds(rows, 32), 0:128] = s[0:32]
            total[pl.ds(rows, 32), 128:256] = s[32:64]
            total[pl.ds(rows, 16), 256:384] = s[64:80]
            total[pl.ds(rows + 16, 16), 256:384] = pltpu.roll(s[64:80], 64, 1)

            @pl.when(q >= 1)
            def _():
                y_to = q - 1

                @pl.when(y_to != yl)
                def _():
                    for c in range(2):
                        y_copy(y_to, c, at(y_to, z, c)).start()

                @pl.when(y_to == yl)
                def _():
                    y_copy(y_to, 0, sibling).start()
                    yr[yl] = total[pl.ds(pl.multiple_of(BLOCK * y_to, 8), BLOCK), :]

    def step(it, carry):
        @pl.when(it < PARTS)
        def _():
            arrived(it, row + xl, None, 0)
            send(it, row + xl, 0, 3, right)
            arrived(it, row + xr, None, 1)
            send(it, row + xr, 1, 4, left)
            arrived(it, other + x, None, 2)
            send(it, other + x, None, 5, right)
            send(it, other + x, None, 6, left)

        @pl.when(it + 1 < PARTS)
        def _():
            send_own(it + 1)

        @pl.when(it >= 1)
        def _():
            q = it - 1
            arrived(q, other + xo, 0, 7)
            arrived(q, other + xo, 1, 8)
            wt[...] += weight_term(q, other)
            pack(q)
            context_term(q, other)

        @pl.when(it < PARTS)
        def _():
            arrived(it, row + xo, 0, 3)
            arrived(it, row + xo, 1, 4)
            wt[...] = weight_term(it, row)
            context_term(it, row)

            @pl.when(it + 1 < PARTS)
            def _():
                prep_w(it + 1)

            @pl.when(it + 2 < PARTS)
            def _():
                prep_grad(it + 2)

            arrived(it, other + xl, None, 5)
            send(it, other + xl, 0, 7, right)
            arrived(it, other + xr, None, 6)
            send(it, other + xr, 1, 8, left)

        @pl.when(it >= 1)
        def _():
            z_stage(it - 1)

        @pl.when(it >= 3)
        def _():
            z_sum(it - 3)

        return carry

    lax.fori_loop(0, PARTS + 1, step, 0)

    def finish(i, carry):
        r = pl.ds(pl.multiple_of(i * CHUNK, CHUNK), CHUNK)
        gcb[r, :] = acc[r, :].astype(jnp.bfloat16)
        return carry

    lax.fori_loop(0, 2 * NX, finish, 0)
    store = pltpu.make_async_copy(gcb, gc_hbm, out_sem)
    store.start()

    def last_sums(q, carry):
        z_sum(q)
        return carry

    lax.fori_loop(PARTS - 2, PARTS, last_sums, 0)

    for s in range(NY):
        @pl.when(jnp.logical_or(jnp.logical_not(owner), yl != s))
        def _():
            pltpu.make_async_copy(yr.at[s], yr.at[s], yrecv.at[s]).wait()

    done = (yr[0] + yr[1]) + (yr[2] + yr[3])
    gw_ref[...] = jnp.where(core == 0, done[0:20], done[20:40])[:, 0:HQ]

    def drain(q, carry):
        whole, half, block = g.at[q, t], g.at[q, t, pl.ds(0, 64)], zs.at[q, 0]
        for event in (0, 1, 2, 5, 6):
            pltpu.make_async_copy(whole, whole, gsend.at[q, event]).wait()
        for event in (3, 4, 7, 8):
            pltpu.make_async_copy(half, half, gsend.at[q, event]).wait()
        pltpu.make_async_copy(cs.at[q], cs.at[q], csend.at[q]).wait()
        for i in range(1, NZ // 2):
            pltpu.make_async_copy(block, block, zsend.at[q, lax.rem(z // 2 + i, NZ // 2)]).wait()

        @pl.when(jnp.logical_not(owner))
        def _():
            pltpu.make_async_copy(block, block, zsend.at[q, z // 2]).wait()

        return carry

    lax.fori_loop(0, PARTS, drain, 0)

    @pl.when(owner)
    def _():
        for y_to in range(NY):
            y_copy(y_to, 0, sibling).wait_send()

            @pl.when(yl != y_to)
            def _():
                y_copy(y_to, 1, sibling).wait_send()

    store.wait()


def shards(out_grad, context, out_weight, dropout_seeds):
    bf16, f32 = jnp.bfloat16, jnp.float32
    dma = pltpu.SemaphoreType.DMA
    hbm = pl.BlockSpec(memory_space=pl.ANY)
    return pl.pallas_call(
        kernel,
        out_shape=(
            jax.ShapeDtypeStruct((2 * NX * CHUNK, HQ), bf16),
            jax.ShapeDtypeStruct((20, HQ), f32),
        ),
        in_specs=[pl.BlockSpec(memory_space=pltpu.SMEM), hbm, hbm, hbm],
        out_specs=(hbm, pl.BlockSpec(memory_space=pltpu.VMEM)),
        scratch_shapes=[
            pltpu.VMEM((CHUNK, DW), bf16),
            pltpu.VMEM((2 * NX * CHUNK, HQ), bf16),
            pltpu.VMEM((DW, HQ), bf16),
            pltpu.VMEM((CHUNK, DW), bf16),
            pltpu.VMEM((PARTS, 2 * NX, CHUNK, PART), bf16),
            pltpu.VMEM((PARTS, PART, HQ), bf16),
            pltpu.VMEM((2 * NX * CHUNK, LANES), bf16),
            pltpu.VMEM((2 * NX * CHUNK, HQ), f32),
            pltpu.VMEM((PART, LANES), f32),
            pltpu.VMEM((NZ // 2, FOLD, 128), f32),
            pltpu.VMEM((PARTS, NZ // 2, FOLD, 128), bf16),
            pltpu.VMEM((PARTS, NZ // 2, FOLD, 128), bf16),
            pltpu.VMEM((PARTS, NZ // 2, FOLD, 128), bf16),
            pltpu.VMEM((PARTS, NZ, FOLD, 128), bf16),
            pltpu.VMEM((NY * BLOCK, LANES), f32),
            pltpu.VMEM((NY, BLOCK, LANES), f32),
            pltpu.VMEM((2 * NX * CHUNK, HQ), bf16),
            dma((3,)),
            dma,
            dma((PARTS, 9)),
            dma((PARTS, 9)),
            dma((PARTS,)),
            dma((PARTS,)),
            dma((PARTS, NZ // 2)),
            dma((PARTS,)),
            dma((NY, 2)),
            dma((NY,)),
        ],
        compiler_params=pltpu.CompilerParams(
            collective_id=0, has_side_effects=True, vmem_limit_bytes=48 * 2**20
        ),
        cost_estimate=pl.CostEstimate(flops=4 * 1024 * DW * HQ, bytes_accessed=4 << 20, transcendentals=0),
    )(dropout_seeds, out_grad, context, out_weight)


def solution(mesh):
    placed = (P(("dp", "tensor"), None), P("dp", "tensor"), P(None, "tensor"), P("dp", None))
    return jax.shard_map(
        shards,
        mesh=mesh,
        in_specs=placed,
        out_specs=(P("dp", "tensor"), P("dp", "tensor")),
        check_vma=False,
    )
```

```python
import functools

import jax
import jax.numpy as jnp
from jax import lax
from jax.experimental import pallas as pl
from jax.experimental.pallas import tpu as pltpu
from jax.sharding import PartitionSpec as P

KEEP_SCALE = 1.0 / 0.9
NX, NY, NZ = 4, 4, 16
CHUNK = 128
DW, HQ = 2560, 320
PARTS, PART = 5, 512
RUN, BLOCK, BLOCK_Y = 8, 40, 640
PICK = BLOCK_Y // PARTS
LANES = 384
FOLD = 80
MESH = pl.DeviceIdType.MESH


def keep_bits(seed_word, position):
    hashed = position * jnp.int32(-1640531535) + seed_word
    hashed = hashed ^ lax.shift_right_logical(hashed, jnp.int32(15))
    hashed = hashed * jnp.int32(-2048144789)
    hashed = hashed ^ lax.shift_right_logical(hashed, jnp.int32(13))
    hashed = hashed * jnp.int32(-1028477387)
    hashed = hashed ^ lax.shift_right_logical(hashed, jnp.int32(16))
    return (hashed & 1023) >= 102


def kernel(
    seed_ref, grad_hbm, ctx_hbm, w_hbm, gc_hbm, gw_ref,
    grad, ctx, w, perm, g, wq, ctxe, acc, wt, own, cs, cr, zs, zr, total, yr, gcb,
    in_sem, out_sem, znews, ynews, gsend, grecv, csend, crecv, zsend, zrecv, ysend, yrecv,
):
    d = lax.axis_index("dp")
    t = lax.axis_index("tensor")
    core = lax.rem(d, 2)
    z = lax.rem(d // 2, NZ)
    yl = d // (2 * NZ)
    yh = t // NX
    x = lax.rem(t, NX)
    row = yh * NX
    other = (1 - yh) * NX
    xr, xl, xo = lax.rem(x + 1, NX), lax.rem(x + 3, NX), lax.rem(x + 2, NX)
    right, left, across = {"tensor": row + xr}, {"tensor": row + xl}, {"tensor": other + x}
    sibling = {"dp": d + 1 - 2 * core}
    owner = lax.rem(z, 2) == core

    def at(y_to, z_to, core_to):
        return {"dp": (y_to * NZ + z_to) * 2 + core_to}

    loads = [
        pltpu.make_async_copy(a, b, in_sem.at[i])
        for i, (a, b) in enumerate((
            (grad_hbm, grad),
            (w_hbm, w),
            (ctx_hbm, ctx.at[pl.ds(0, HQ)]),
            (ctx_hbm.at[pl.ds(256, 64)], ctx.at[pl.ds(HQ, 64)]),
        ))
    ]
    for load in loads:
        load.start()

    barrier = pltpu.get_barrier_semaphore()

    def greet(device):
        pl.semaphore_signal(barrier, inc=1, device_id=device, device_id_type=MESH)

    def y_next(i):
        return at(lax.rem(yl + i + NY, NY), z, core)

    def z_next(i):
        return at(yl, lax.rem(z + i + NZ, NZ), core)

    greeted = (across, right, left, z_next(1), z_next(-1), y_next(1), y_next(-1), sibling)
    for device in greeted:
        greet(device)

    def tell(sem, devices):
        for device in devices:
            pl.semaphore_signal(sem, inc=1, device_id=device, device_id_type=MESH)

    def tell_near():
        tell(znews.at[0], (z_next(1), z_next(-1)))
        tell(ynews.at[0], (y_next(1), y_next(-1)))

    def tell_two():
        pl.semaphore_wait(znews.at[0], 2)
        tell(znews.at[1], (z_next(2), z_next(-2)))
        pl.semaphore_wait(ynews.at[0], 2)
        tell(ynews.at[1], (y_next(1), y_next(-1)))

    def tell_four():
        pl.semaphore_wait(znews.at[1], 2)
        tell(znews.at[2], (z_next(4), z_next(-4)))
        pl.semaphore_wait(ynews.at[1], 2)

    def all_in():
        pl.semaphore_wait(znews.at[2], 2)

    seed = seed_ref[0, 0]

    def feature_in_block(q, index):
        half, j = index // (PICK // 2), lax.rem(index // RUN, NZ // 2)
        return BLOCK * (2 * j + half) + RUN * q + lax.rem(index, RUN)

    def onehot(q):
        feature = feature_in_block(q, lax.broadcasted_iota(jnp.int32, (PICK, 1), 0))
        columns = lax.broadcasted_iota(jnp.int32, (PICK, BLOCK_Y), 1)
        perm[PICK * q:PICK * (q + 1)] = jnp.where(columns == feature, 1.0, 0.0).astype(jnp.bfloat16)

    def picked(a, p):
        return lax.dot_general(a, p, (((1,), (1,)), ((), ())), preferred_element_type=jnp.float32)

    first_position = (t * CHUNK + lax.broadcasted_iota(jnp.int32, (CHUNK, 1), 0)) * DW

    def prep_grad(parts):
        for y in range(NY):
            block = grad[:, BLOCK_Y * y:BLOCK_Y * (y + 1)]
            scaled = picked(block, perm[PICK * parts[0]:PICK * (parts[-1] + 1)]) * KEEP_SCALE
            for i, q in enumerate(parts):
                feature = feature_in_block(q, lax.broadcasted_iota(jnp.int32, (1, PICK), 1))
                keep = keep_bits(seed, first_position + (feature + y * BLOCK_Y))
                kept = jnp.where(keep, scaled[:, PICK * i:PICK * (i + 1)], 0.0)
                g[q, t, :, PICK * y:PICK * (y + 1)] = kept.astype(jnp.bfloat16)

    def prep_w():
        for y in range(NY):
            columns = picked(w[:, BLOCK_Y * y:BLOCK_Y * (y + 1)], perm[...]).astype(jnp.bfloat16)
            for q in range(PARTS):
                wq[q, :, PICK * y:PICK * (y + 1)] = columns[:, PICK * q:PICK * (q + 1)]

    whole, low, high = (0, 128), (0, 64), (64, 64)

    def piece(n, origin, rows):
        return g.at[n, origin, pl.ds(*rows)]

    def send(n, origin, rows, event, device):
        ref = piece(n, origin, rows)
        pltpu.make_async_remote_copy(
            src_ref=ref, dst_ref=ref, send_sem=gsend.at[n, event], recv_sem=grecv.at[n, event],
            device_id=device, device_id_type=MESH,
        ).start()

    def arrived(n, origin, rows, event):
        ref = piece(n, origin, rows)
        pltpu.make_async_copy(ref, ref, grecv.at[n, event]).wait()

    def sent(n, rows, event):
        ref = piece(n, t, rows)
        pltpu.make_async_copy(ref, ref, gsend.at[n, event]).wait()

    def send_own(n):
        send(n, t, whole, 0, right)
        send(n, t, whole, 1, left)

    def send_across(n):
        send(n, t, whole, 2, across)

    def relay_row(n):
        arrived(n, row + xl, whole, 0)
        send(n, row + xl, low, 3, right)
        arrived(n, row + xr, whole, 1)
        send(n, row + xr, high, 4, left)

    def relay_across(n):
        arrived(n, other + x, whole, 2)
        send(n, other + x, whole, 5, right)
        send(n, other + x, whole, 6, left)

    def relay_other(n):
        arrived(n, other + xl, whole, 5)
        send(n, other + xl, low, 7, right)
        arrived(n, other + xr, whole, 6)
        send(n, other + xr, high, 8, left)

    onehot(0)
    loads[0].wait()
    prep_grad((0,))
    pl.semaphore_wait(barrier, len(greeted))
    send_across(0)
    send_own(0)
    tell_near()
    for q in range(1, PARTS):
        onehot(q)
    prep_grad((1, 2))
    send_across(1)
    prep_grad((3, 4))
    sent(0, whole, 0)
    sent(0, whole, 1)
    send_own(1)
    relay_row(0)
    relay_across(0)

    def prepare():
        loads[1].wait()
        prep_w()
        loads[2].wait()
        loads[3].wait()
        for i in range(2 * NX):
            tokens = slice(i * CHUNK, (i + 1) * CHUNK)
            ctxe[tokens, :] = ctx[:, tokens].T
        acc[...] = jnp.zeros_like(acc)

    def rows_of(q, start):
        return g[q, pl.ds(start, NX)].reshape(NX * CHUNK, PART)

    def weight_term(q, start):
        tokens = pl.ds(pl.multiple_of(start * CHUNK, NX * CHUNK), NX * CHUNK)
        return lax.dot_general(
            rows_of(q, start), ctxe[tokens, :], (((0,), (0,)), ((), ())),
            preferred_element_type=jnp.float32,
        )

    def context_term(q, start):
        tokens = pl.ds(pl.multiple_of(start * CHUNK, NX * CHUNK), NX * CHUNK)
        acc[:, tokens] += picked(wq[q], rows_of(q, start))

    low_lanes = lax.broadcasted_iota(jnp.int32, (16, 128), 1) < 64

    def folded(half, j):
        runs = [
            pl.ds(pl.multiple_of(y * PICK + half * (PICK // 2) + j * RUN, RUN), RUN) for y in range(NY)
        ]
        last = [wt[run, 256:384] for run in runs]
        return (
            jnp.concatenate([wt[run, 0:128] for run in runs], axis=0),
            jnp.concatenate([wt[run, 128:256] for run in runs], axis=0),
            jnp.where(low_lanes, jnp.concatenate(last[:2], axis=0), jnp.concatenate(last[2:], axis=0)),
        )

    def pack(q):
        def body(j, carry):
            a, b, c = folded(1 - core, j)
            cs[q, j, 0:32] = a.astype(jnp.bfloat16)
            cs[q, j, 32:64] = b.astype(jnp.bfloat16)
            cs[q, j, 64:80] = c.astype(jnp.bfloat16)
            return carry

        lax.fori_loop(0, NZ // 2, body, 0)
        to_sibling(q).start()

        def mine(j, carry):
            a, b, c = folded(core, j)
            own[j, 0:32], own[j, 32:64], own[j, 64:80] = a, b, c
            return carry

        lax.fori_loop(0, NZ // 2, mine, 0)

    def to_sibling(q):
        return pltpu.make_async_remote_copy(
            src_ref=cs.at[q], dst_ref=cr.at[q], send_sem=csend.at[q], recv_sem=crecv.at[q],
            device_id=sibling, device_id_type=MESH,
        )

    def z_copy(q, j):
        return pltpu.make_async_remote_copy(
            src_ref=zs.at[q, j], dst_ref=zr.at[q, z], send_sem=zsend.at[q, j], recv_sem=zrecv.at[q],
            device_id=at(yl, 2 * j + core, core), device_id_type=MESH,
        )

    def z_stage(q):
        to_sibling(q).wait_recv()

        def body(j, carry):
            zs[q, j] = (own[j] + cr[q, j].astype(jnp.float32)).astype(jnp.bfloat16)
            return carry

        lax.fori_loop(0, NZ // 2, body, 0)
        for i in (4, 3, 5, 2, 6, 1, 7):
            z_copy(q, lax.rem(z // 2 + i, NZ // 2)).start()

        @pl.when(owner)
        def _():
            pltpu.make_async_copy(zs.at[q, z // 2], zr.at[q, z], zrecv.at[q]).start()

        @pl.when(jnp.logical_not(owner))
        def _():
            z_copy(q, z // 2).start()

    def y_copy(q, y_to, core_to, device):
        return pltpu.make_async_remote_copy(
            src_ref=total.at[q, y_to], dst_ref=yr.at[yl, q],
            send_sem=ysend.at[q, y_to, core_to], recv_sem=yrecv.at[yl, q],
            device_id=device, device_id_type=MESH,
        )

    def wanted(q, core_to):
        return q <= 2 if core_to == 0 else q >= 2

    def z_sum(q):
        @pl.when(owner)
        def _():
            pltpu.make_async_copy(zr.at[q], zr.at[q], zrecv.at[q]).wait()
            s = zr[q, 0].astype(jnp.float32)
            for i in range(1, NZ):
                s = s + zr[q, i].astype(jnp.float32)
            rolled = pltpu.roll(s[64:80], 64, 1)
            for y in range(NY):
                total[q, y, :, 0:128] = s[RUN * y:RUN * (y + 1)]
                total[q, y, :, 128:256] = s[32 + RUN * y:32 + RUN * (y + 1)]
                last = s[64:80] if y < 2 else rolled
                total[q, y, :, 256:384] = last[RUN * (y % 2):RUN * (y % 2 + 1)]
            yr[yl, q] = total[q, yl]
            for c in range(2):
                @pl.when(wanted(q, c))
                def _():
                    for i in (2, 1, 3):
                        y_to = lax.rem(yl + i, NY)
                        y_copy(q, y_to, c, at(y_to, z, c)).start()

                    @pl.when(core != c)
                    def _():
                        y_copy(q, yl, c, sibling).start()

    prepare()
    tell_two()

    def step(n, carry):
        arrived(n, row + xo, low, 3)
        arrived(n, row + xo, high, 4)
        wt[...] = weight_term(n, row)
        context_term(n, row)
        relay_other(n)

        @pl.when(n == 0)
        def _():
            tell_four()

        @pl.when(n + 2 < PARTS)
        def _():
            send_across(n + 2)

        sent(n, low, 7)
        sent(n, low, 8)

        @pl.when(n + 1 < PARTS)
        def _():
            relay_row(n + 1)
            relay_across(n + 1)

        arrived(n, other + xo, low, 7)
        arrived(n, other + xo, high, 8)
        wt[...] += weight_term(n, other)
        pack(n)
        context_term(n, other)

        @pl.when(n + 1 < PARTS)
        def _():
            sent(n + 1, low, 3)
            sent(n + 1, low, 4)

        @pl.when(n + 2 < PARTS)
        def _():
            send_own(n + 2)

        @pl.when(n == 0)
        def _():
            all_in()

        z_stage(n)

        @pl.when(n >= 2)
        def _():
            z_sum(n - 2)

        return carry

    lax.fori_loop(0, PARTS, step, 0)

    gcb[...] = acc[...].astype(jnp.bfloat16)
    store = pltpu.make_async_copy(gcb, gc_hbm, out_sem)
    store.start()

    def last_sums(q, carry):
        z_sum(q)
        return carry

    lax.fori_loop(PARTS - 2, PARTS, last_sums, 0)

    def collect(q, carry):
        @pl.when(jnp.where(core == 0, q <= 2, q >= 2))
        def _():
            for s in range(NY):
                @pl.when(jnp.logical_or(jnp.logical_not(owner), yl != s))
                def _():
                    pltpu.make_async_copy(yr.at[s, q], yr.at[s, q], yrecv.at[s, q]).wait()

        return carry

    lax.fori_loop(0, PARTS, collect, 0)
    rows = []
    for i in range(3):
        q = 2 * core + i
        rows.append((yr[0, q] + yr[1, q]) + (yr[2, q] + yr[3, q]))
    done = jnp.concatenate(rows, axis=0)
    gw_ref[...] = jnp.where(core == 0, done[0:20], done[4:24])[:, 0:HQ]

    def drain(q, carry):
        block = zs.at[q, 0]
        for event in (2, 5, 6):
            sent(q, whole, event)

        @pl.when(q == 0)
        def _():
            sent(q, low, 3)
            sent(q, low, 4)

        @pl.when(q >= 1)
        def _():
            sent(q, whole, 0)
            sent(q, whole, 1)

        pltpu.make_async_copy(cs.at[q], cs.at[q], csend.at[q]).wait()
        for i in range(1, NZ // 2):
            pltpu.make_async_copy(block, block, zsend.at[q, lax.rem(z // 2 + i, NZ // 2)]).wait()

        @pl.when(jnp.logical_not(owner))
        def _():
            pltpu.make_async_copy(block, block, zsend.at[q, z // 2]).wait()

        return carry

    lax.fori_loop(0, PARTS, drain, 0)

    @pl.when(owner)
    def _():
        def drain_y(q, carry):
            for c in range(2):
                @pl.when(wanted(q, c))
                def _():
                    for y_to in range(NY):
                        @pl.when(jnp.logical_or(yl != y_to, core != c))
                        def _():
                            y_copy(q, y_to, c, sibling).wait_send()

            return carry

        lax.fori_loop(0, PARTS, drain_y, 0)

    store.wait()


def hand_over(a_ref, b_ref, a_out, b_out):
    a_out[...] = a_ref[...]
    b_out[...] = b_ref[...]


def shards(out_grad, context, out_weight, dropout_seeds):
    bf16, f32 = jnp.bfloat16, jnp.float32
    dma = pltpu.SemaphoreType.DMA
    hbm = pl.BlockSpec(memory_space=pltpu.HBM)
    tokens = 2 * NX * CHUNK
    grad_ctx, weight_grad = pl.pallas_call(
        kernel,
        out_shape=(
            jax.ShapeDtypeStruct((HQ, tokens), bf16),
            jax.ShapeDtypeStruct((20, HQ), f32),
        ),
        in_specs=[pl.BlockSpec(memory_space=pltpu.SMEM), hbm, hbm, hbm],
        out_specs=(hbm, pl.BlockSpec(memory_space=pltpu.VMEM)),
        scratch_shapes=[
            pltpu.VMEM((CHUNK, DW), bf16),
            pltpu.VMEM((LANES, tokens), bf16),
            pltpu.VMEM((HQ, DW), bf16),
            pltpu.VMEM((BLOCK_Y, BLOCK_Y), bf16),
            pltpu.VMEM((PARTS, 2 * NX, CHUNK, PART), bf16),
            pltpu.VMEM((PARTS, HQ, PART), bf16),
            pltpu.VMEM((tokens, LANES), bf16),
            pltpu.VMEM((HQ, tokens), f32),
            pltpu.VMEM((PART, LANES), f32),
            pltpu.VMEM((NZ // 2, FOLD, 128), f32),
            pltpu.VMEM((PARTS, NZ // 2, FOLD, 128), bf16),
            pltpu.VMEM((PARTS, NZ // 2, FOLD, 128), bf16),
            pltpu.VMEM((PARTS, NZ // 2, FOLD, 128), bf16),
            pltpu.VMEM((PARTS, NZ, FOLD, 128), bf16),
            pltpu.VMEM((PARTS, NY, RUN, LANES), f32),
            pltpu.VMEM((NY, PARTS, RUN, LANES), f32),
            pltpu.VMEM((HQ, tokens), bf16),
            dma((4,)),
            dma,
            pltpu.SemaphoreType.REGULAR((3,)),
            pltpu.SemaphoreType.REGULAR((2,)),
            dma((PARTS, 9)),
            dma((PARTS, 9)),
            dma((PARTS,)),
            dma((PARTS,)),
            dma((PARTS, NZ // 2)),
            dma((PARTS,)),
            dma((PARTS, NY, 2)),
            dma((NY, PARTS)),
        ],
        compiler_params=pltpu.CompilerParams(
            collective_id=0, has_side_effects=True, vmem_limit_bytes=56 * 2**20
        ),
        cost_estimate=pl.CostEstimate(flops=4 * tokens * DW * HQ, bytes_accessed=4 << 20, transcendentals=0),
    )(dropout_seeds, out_grad, context.T, out_weight.T)
    grad_ctx, weight_grad = pl.pallas_call(
        hand_over,
        out_shape=(
            jax.ShapeDtypeStruct((HQ, tokens), bf16),
            jax.ShapeDtypeStruct((20, HQ), f32),
        ),
        in_specs=[pl.BlockSpec(memory_space=pltpu.VMEM)] * 2,
        out_specs=[pl.BlockSpec(memory_space=pltpu.VMEM)] * 2,
        cost_estimate=pl.CostEstimate(flops=0, bytes_accessed=2 << 20, transcendentals=0),
    )(grad_ctx, weight_grad)
    return grad_ctx.T, weight_grad


def solution(mesh):
    placed = (P(("dp", "tensor"), None), P("dp", "tensor"), P(None, "tensor"), P("dp", None))
    return jax.shard_map(
        shards,
        mesh=mesh,
        in_specs=placed,
        out_specs=(P("dp", "tensor"), P("dp", "tensor")),
        check_vma=False,
    )
```

```python
import functools

import jax
import jax.numpy as jnp
from jax import lax
from jax.experimental import pallas as pl
from jax.experimental.pallas import tpu as pltpu
from jax.sharding import PartitionSpec as P

KEEP_SCALE = 1.0 / 0.9
NX, NY, NZ = 4, 4, 16
CHUNK = 128
DW, HQ = 2560, 320
PARTS, PART = 5, 512
RUN, BLOCK, BLOCK_Y = 8, 40, 640
LAST = PARTS - 1
PICK = BLOCK_Y // PARTS
LANES = 384
FOLD = 80
MESH = pl.DeviceIdType.MESH


def keep_bits(seed_word, position):
    hashed = position * jnp.int32(-1640531535) + seed_word
    hashed = hashed ^ lax.shift_right_logical(hashed, jnp.int32(15))
    hashed = hashed * jnp.int32(-2048144789)
    hashed = hashed ^ lax.shift_right_logical(hashed, jnp.int32(13))
    hashed = hashed * jnp.int32(-1028477387)
    hashed = hashed ^ lax.shift_right_logical(hashed, jnp.int32(16))
    return (hashed & 1023) >= 102


def kernel(
    seed_ref, grad_hbm, ctx_hbm, w_hbm, gc_hbm, gw_ref,
    grad, ctx, w, perm, g, wq, ctxe, acc, wt, own, cs, cr, zs, zr, total, yr, gcb,
    in_sem, out_sem, znews, ynews, gsend, grecv, csend, crecv, zsend, zrecv, ysend, yrecv,
):
    d = lax.axis_index("dp")
    t = lax.axis_index("tensor")
    core = lax.rem(d, 2)
    z = lax.rem(d // 2, NZ)
    yl = d // (2 * NZ)
    yh = t // NX
    x = lax.rem(t, NX)
    row = yh * NX
    other = (1 - yh) * NX
    xr, xl, xo = lax.rem(x + 1, NX), lax.rem(x + 3, NX), lax.rem(x + 2, NX)
    right, left, across = {"tensor": row + xr}, {"tensor": row + xl}, {"tensor": other + x}
    sibling = {"dp": d + 1 - 2 * core}
    owner = lax.rem(z, 2) == core

    def at(y_to, z_to, core_to):
        return {"dp": (y_to * NZ + z_to) * 2 + core_to}

    loads = [
        pltpu.make_async_copy(a, b, in_sem.at[i])
        for i, (a, b) in enumerate((
            (grad_hbm, grad),
            (w_hbm, w),
            (ctx_hbm, ctx.at[pl.ds(0, HQ)]),
            (ctx_hbm.at[pl.ds(256, 64)], ctx.at[pl.ds(HQ, 64)]),
        ))
    ]
    loads[0].start()

    barrier = pltpu.get_barrier_semaphore()

    def greet(device):
        pl.semaphore_signal(barrier, inc=1, device_id=device, device_id_type=MESH)

    def y_next(i):
        return at(lax.rem(yl + i + NY, NY), z, core)

    def z_next(i):
        return at(yl, lax.rem(z + i + NZ, NZ), core)

    greeted = (across, right, left, z_next(1), z_next(-1), y_next(1), y_next(-1), sibling)
    for device in greeted:
        greet(device)

    def tell(sem, devices):
        for device in devices:
            pl.semaphore_signal(sem, inc=1, device_id=device, device_id_type=MESH)

    def tell_near():
        tell(znews.at[0], (z_next(1), z_next(-1)))
        tell(ynews.at[0], (y_next(1), y_next(-1)))

    def tell_two():
        pl.semaphore_wait(znews.at[0], 2)
        tell(znews.at[1], (z_next(2), z_next(-2)))
        pl.semaphore_wait(ynews.at[0], 2)
        tell(ynews.at[1], (y_next(1), y_next(-1)))

    def tell_four():
        pl.semaphore_wait(znews.at[1], 2)
        tell(znews.at[2], (z_next(4), z_next(-4)))
        pl.semaphore_wait(ynews.at[1], 2)

    def all_in():
        pl.semaphore_wait(znews.at[2], 2)

    seed = seed_ref[0, 0]

    def feature_in_block(q, index):
        half, j = index // (PICK // 2), lax.rem(index // RUN, NZ // 2)
        return BLOCK * (2 * j + half) + RUN * q + lax.rem(index, RUN)

    def onehot(q):
        feature = feature_in_block(q, lax.broadcasted_iota(jnp.int32, (PICK, 1), 0))
        columns = lax.broadcasted_iota(jnp.int32, (PICK, BLOCK_Y), 1)
        perm[PICK * q:PICK * (q + 1)] = jnp.where(columns == feature, 1.0, 0.0).astype(jnp.bfloat16)

    def picked(a, p):
        return lax.dot_general(a, p, (((1,), (1,)), ((), ())), preferred_element_type=jnp.float32)

    first_position = (t * CHUNK + lax.broadcasted_iota(jnp.int32, (CHUNK, 1), 0)) * DW

    def prep_grad(parts):
        for y in range(NY):
            block = grad[:, BLOCK_Y * y:BLOCK_Y * (y + 1)]
            scaled = picked(block, perm[PICK * parts[0]:PICK * (parts[-1] + 1)]) * KEEP_SCALE
            for i, q in enumerate(parts):
                feature = feature_in_block(q, lax.broadcasted_iota(jnp.int32, (1, PICK), 1))
                keep = keep_bits(seed, first_position + (feature + y * BLOCK_Y))
                kept = jnp.where(keep, scaled[:, PICK * i:PICK * (i + 1)], 0.0)
                g[q, t, :, PICK * y:PICK * (y + 1)] = kept.astype(jnp.bfloat16)

    def prep_w():
        for y in range(NY):
            columns = picked(w[:, BLOCK_Y * y:BLOCK_Y * (y + 1)], perm[...]).astype(jnp.bfloat16)
            for q in range(PARTS):
                wq[q, :, PICK * y:PICK * (y + 1)] = columns[:, PICK * q:PICK * (q + 1)]

    whole, low, high = (0, 128), (0, 64), (64, 64)

    def piece(n, origin, rows):
        return g.at[n, origin, pl.ds(*rows)]

    def send(n, origin, rows, event, device):
        ref = piece(n, origin, rows)
        pltpu.make_async_remote_copy(
            src_ref=ref, dst_ref=ref, send_sem=gsend.at[n, event], recv_sem=grecv.at[n, event],
            device_id=device, device_id_type=MESH,
        ).start()

    def arrived(n, origin, rows, event):
        ref = piece(n, origin, rows)
        pltpu.make_async_copy(ref, ref, grecv.at[n, event]).wait()

    def sent(n, rows, event):
        ref = piece(n, t, rows)
        pltpu.make_async_copy(ref, ref, gsend.at[n, event]).wait()

    def send_own(n):
        send(n, t, whole, 0, right)
        send(n, t, whole, 1, left)

    def send_across(n):
        send(n, t, whole, 2, across)

    def relay_row(n):
        arrived(n, row + xl, whole, 0)
        send(n, row + xl, low, 3, right)
        arrived(n, row + xr, whole, 1)
        send(n, row + xr, high, 4, left)

    def relay_across(n):
        arrived(n, other + x, whole, 2)
        send(n, other + x, whole, 5, right)
        send(n, other + x, whole, 6, left)

    def relay_other(n):
        arrived(n, other + xl, whole, 5)
        send(n, other + xl, low, 7, right)
        arrived(n, other + xr, whole, 6)
        send(n, other + xr, high, 8, left)

    onehot(0)
    loads[0].wait()
    for load in loads[1:]:
        load.start()
    prep_grad((0,))
    pl.semaphore_wait(barrier, len(greeted))
    send_across(0)
    send_own(0)
    tell_near()
    for q in range(1, PARTS):
        onehot(q)
    prep_grad((1, 2))
    send_across(1)
    prep_grad((3, 4))
    sent(0, whole, 0)
    sent(0, whole, 1)
    send_own(1)
    relay_row(0)
    send_own(2)
    relay_across(0)

    def prepare():
        loads[1].wait()
        prep_w()
        loads[2].wait()
        loads[3].wait()
        for i in range(2 * NX):
            tokens = slice(i * CHUNK, (i + 1) * CHUNK)
            ctxe[tokens, :] = ctx[:, tokens].T
        acc[...] = jnp.zeros_like(acc)

    def rows_of(q, start):
        return g[q, pl.ds(start, NX)].reshape(NX * CHUNK, PART)

    def weight_term(q, start):
        tokens = pl.ds(pl.multiple_of(start * CHUNK, NX * CHUNK), NX * CHUNK)
        return lax.dot_general(
            rows_of(q, start), ctxe[tokens, :], (((0,), (0,)), ((), ())),
            preferred_element_type=jnp.float32,
        )

    def context_term(q, start):
        tokens = pl.ds(pl.multiple_of(start * CHUNK, NX * CHUNK), NX * CHUNK)
        acc[:, tokens] += picked(wq[q], rows_of(q, start))

    low_lanes = lax.broadcasted_iota(jnp.int32, (16, 128), 1) < 64

    def folded(half, j):
        runs = [
            pl.ds(pl.multiple_of(y * PICK + half * (PICK // 2) + j * RUN, RUN), RUN) for y in range(NY)
        ]
        last = [wt[run, 256:384] for run in runs]
        return (
            jnp.concatenate([wt[run, 0:128] for run in runs], axis=0),
            jnp.concatenate([wt[run, 128:256] for run in runs], axis=0),
            jnp.where(low_lanes, jnp.concatenate(last[:2], axis=0), jnp.concatenate(last[2:], axis=0)),
        )

    def pack(q):
        for j in range(NZ // 2):
            a, b, c = folded(1 - core, j)
            cs[q, j, 0:32] = a.astype(jnp.bfloat16)
            cs[q, j, 32:64] = b.astype(jnp.bfloat16)
            cs[q, j, 64:80] = c.astype(jnp.bfloat16)
        to_sibling(q).start()
        for j in range(NZ // 2):
            own[j, 0:32], own[j, 32:64], own[j, 64:80] = folded(core, j)

    def to_sibling(q):
        return pltpu.make_async_remote_copy(
            src_ref=cs.at[q], dst_ref=cr.at[q], send_sem=csend.at[q], recv_sem=crecv.at[q],
            device_id=sibling, device_id_type=MESH,
        )

    def z_copy(q, j):
        return pltpu.make_async_remote_copy(
            src_ref=zs.at[q, j], dst_ref=zr.at[q, z], send_sem=zsend.at[q, j], recv_sem=zrecv.at[q],
            device_id=at(yl, 2 * j + core, core), device_id_type=MESH,
        )

    def z_stage(q):
        to_sibling(q).wait_recv()

        for j in range(NZ // 2):
            zs[q, j] = (own[j] + cr[q, j].astype(jnp.float32)).astype(jnp.bfloat16)
        for i in (4, 3, 5, 2, 6, 1, 7):
            z_copy(q, lax.rem(z // 2 + i, NZ // 2)).start()

        @pl.when(owner)
        def _():
            pltpu.make_async_copy(zs.at[q, z // 2], zr.at[q, z], zrecv.at[q]).start()

        @pl.when(jnp.logical_not(owner))
        def _():
            z_copy(q, z // 2).start()

    def y_copy(q, y_to, core_to, device):
        return pltpu.make_async_remote_copy(
            src_ref=total.at[q, y_to], dst_ref=yr.at[yl, q],
            send_sem=ysend.at[q, y_to, core_to], recv_sem=yrecv.at[yl, q],
            device_id=device, device_id_type=MESH,
        )

    def wanted(q, core_to):
        return q <= 2 if core_to == 0 else q >= 2

    def z_sum(q):
        @pl.when(owner)
        def _():
            pltpu.make_async_copy(zr.at[q], zr.at[q], zrecv.at[q]).wait()
            s = zr[q, 0].astype(jnp.float32)
            for i in range(1, NZ):
                s = s + zr[q, i].astype(jnp.float32)
            rolled = pltpu.roll(s[64:80], 64, 1)
            for y in range(NY):
                total[q, y, :, 0:128] = s[RUN * y:RUN * (y + 1)]
                total[q, y, :, 128:256] = s[32 + RUN * y:32 + RUN * (y + 1)]
                last = s[64:80] if y < 2 else rolled
                total[q, y, :, 256:384] = last[RUN * (y % 2):RUN * (y % 2 + 1)]
            yr[yl, q] = total[q, yl]
            for c in range(2):
                @pl.when(wanted(q, c))
                def _():
                    for i in (2, 1, 3):
                        y_to = lax.rem(yl + i, NY)
                        y_copy(q, y_to, c, at(y_to, z, c)).start()

                    @pl.when(core != c)
                    def _():
                        y_copy(q, yl, c, sibling).start()

    prepare()
    tell_two()

    def step(n, carry):
        relay_other(n)

        @pl.when(n == 0)
        def _():
            tell_four()

        arrived(n, row + xo, low, 3)
        arrived(n, row + xo, high, 4)
        wt[...] = weight_term(n, row)
        context_term(n, row)

        @pl.when(n + 1 < PARTS)
        def _():
            relay_row(n + 1)

        @pl.when(n + 2 < PARTS)
        def _():
            send_across(n + 2)

        @pl.when(n + 1 < PARTS)
        def _():
            relay_across(n + 1)

        arrived(n, other + xo, low, 7)
        arrived(n, other + xo, high, 8)
        wt[...] += weight_term(n, other)
        pack(n)
        context_term(n, other)

        @pl.when(n + 3 < PARTS)
        def _():
            send_own(n + 3)

        @pl.when(n == 0)
        def _():
            all_in()

        z_stage(n)

        @pl.when(n >= 2)
        def _():
            z_sum(n - 2)

        return carry

    lax.fori_loop(0, PARTS, step, 0)

    gcb[...] = acc[...].astype(jnp.bfloat16)
    store = pltpu.make_async_copy(gcb, gc_hbm, out_sem)
    store.start()

    z_sum(LAST - 1)

    def drain_z(q):
        block = zs.at[q, 0]
        for i in range(1, NZ // 2):
            pltpu.make_async_copy(block, block, zsend.at[q, lax.rem(z // 2 + i, NZ // 2)]).wait()

        @pl.when(jnp.logical_not(owner))
        def _():
            pltpu.make_async_copy(block, block, zsend.at[q, z // 2]).wait()

    def drain_y(q):
        for c in range(2):
            @pl.when(jnp.logical_and(owner, wanted(q, c)))
            def _():
                for y_to in range(NY):
                    @pl.when(jnp.logical_or(yl != y_to, core != c))
                    def _():
                        y_copy(q, y_to, c, sibling).wait_send()

    def drain(q, carry):
        for event in (2, 5, 6):
            sent(q, whole, event)
        for event in (3, 4, 7, 8):
            sent(q, low, event)

        @pl.when(q >= 1)
        def _():
            sent(q, whole, 0)
            sent(q, whole, 1)

        pltpu.make_async_copy(cs.at[q], cs.at[q], csend.at[q]).wait()

        @pl.when(q < LAST)
        def _():
            drain_z(q)
            drain_y(q)

        return carry

    lax.fori_loop(0, PARTS, drain, 0)
    z_sum(LAST)
    drain_z(LAST)
    store.wait()

    def collect(q, carry):
        @pl.when(jnp.where(core == 0, q <= 2, q >= 2))
        def _():
            for s in range(NY):
                @pl.when(jnp.logical_or(jnp.logical_not(owner), yl != s))
                def _():
                    pltpu.make_async_copy(yr.at[s, q], yr.at[s, q], yrecv.at[s, q]).wait()

        return carry

    lax.fori_loop(0, PARTS, collect, 0)
    rows = []
    for i in range(3):
        q = 2 * core + i
        rows.append((yr[0, q] + yr[1, q]) + (yr[2, q] + yr[3, q]))
    done = jnp.concatenate(rows, axis=0)
    gw_ref[...] = jnp.where(core == 0, done[0:20], done[4:24])[:, 0:HQ]

    drain_y(LAST)


def hand_over(a_ref, b_ref, a_out, b_out):
    a_out[...] = a_ref[...]
    b_out[...] = b_ref[...]


def shards(out_grad, context, out_weight, dropout_seeds):
    bf16, f32 = jnp.bfloat16, jnp.float32
    dma = pltpu.SemaphoreType.DMA
    hbm = pl.BlockSpec(memory_space=pltpu.HBM)
    tokens = 2 * NX * CHUNK
    grad_ctx, weight_grad = pl.pallas_call(
        kernel,
        out_shape=(
            jax.ShapeDtypeStruct((HQ, tokens), bf16),
            jax.ShapeDtypeStruct((20, HQ), f32),
        ),
        in_specs=[pl.BlockSpec(memory_space=pltpu.SMEM), hbm, hbm, hbm],
        out_specs=(hbm, pl.BlockSpec(memory_space=pltpu.VMEM)),
        scratch_shapes=[
            pltpu.VMEM((CHUNK, DW), bf16),
            pltpu.VMEM((LANES, tokens), bf16),
            pltpu.VMEM((HQ, DW), bf16),
            pltpu.VMEM((BLOCK_Y, BLOCK_Y), bf16),
            pltpu.VMEM((PARTS, 2 * NX, CHUNK, PART), bf16),
            pltpu.VMEM((PARTS, HQ, PART), bf16),
            pltpu.VMEM((tokens, LANES), bf16),
            pltpu.VMEM((HQ, tokens), f32),
            pltpu.VMEM((PART, LANES), f32),
            pltpu.VMEM((NZ // 2, FOLD, 128), f32),
            pltpu.VMEM((PARTS, NZ // 2, FOLD, 128), bf16),
            pltpu.VMEM((PARTS, NZ // 2, FOLD, 128), bf16),
            pltpu.VMEM((PARTS, NZ // 2, FOLD, 128), bf16),
            pltpu.VMEM((PARTS, NZ, FOLD, 128), bf16),
            pltpu.VMEM((PARTS, NY, RUN, LANES), f32),
            pltpu.VMEM((NY, PARTS, RUN, LANES), f32),
            pltpu.VMEM((HQ, tokens), bf16),
            dma((4,)),
            dma,
            pltpu.SemaphoreType.REGULAR((3,)),
            pltpu.SemaphoreType.REGULAR((2,)),
            dma((PARTS, 9)),
            dma((PARTS, 9)),
            dma((PARTS,)),
            dma((PARTS,)),
            dma((PARTS, NZ // 2)),
            dma((PARTS,)),
            dma((PARTS, NY, 2)),
            dma((NY, PARTS)),
        ],
        compiler_params=pltpu.CompilerParams(
            collective_id=0, has_side_effects=True, vmem_limit_bytes=56 * 2**20
        ),
        cost_estimate=pl.CostEstimate(flops=4 * tokens * DW * HQ, bytes_accessed=4 << 20, transcendentals=0),
    )(dropout_seeds, out_grad, context.T, out_weight.T)
    grad_ctx, weight_grad = pl.pallas_call(
        hand_over,
        out_shape=(
            jax.ShapeDtypeStruct((HQ, tokens), bf16),
            jax.ShapeDtypeStruct((20, HQ), f32),
        ),
        in_specs=[pl.BlockSpec(memory_space=pltpu.VMEM)] * 2,
        out_specs=[pl.BlockSpec(memory_space=pltpu.VMEM)] * 2,
        cost_estimate=pl.CostEstimate(flops=0, bytes_accessed=2 << 20, transcendentals=0),
    )(grad_ctx, weight_grad)
    return grad_ctx.T, weight_grad


def solution(mesh):
    placed = (P(("dp", "tensor"), None), P("dp", "tensor"), P(None, "tensor"), P("dp", None))
    return jax.shard_map(
        shards,
        mesh=mesh,
        in_specs=placed,
        out_specs=(P("dp", "tensor"), P("dp", "tensor")),
        check_vma=False,
    )
```

```python
import functools

import jax
import jax.numpy as jnp
from jax import lax
from jax.experimental import pallas as pl
from jax.experimental.pallas import tpu as pltpu
from jax.sharding import PartitionSpec as P

KEEP_SCALE = 1.0 / 0.9
NX, NY, NZ = 4, 4, 16
CHUNK = 128
DW, HQ = 2560, 320
PARTS, PART = 5, 512
RUN, BLOCK, BLOCK_Y = 8, 40, 640
LAST = PARTS - 1
PICK = BLOCK_Y // PARTS
LANES = 384
FOLD = 80
MESH = pl.DeviceIdType.MESH


def keep_bits(seed_word, position):
    hashed = position * jnp.int32(-1640531535) + seed_word
    hashed = hashed ^ lax.shift_right_logical(hashed, jnp.int32(15))
    hashed = hashed * jnp.int32(-2048144789)
    hashed = hashed ^ lax.shift_right_logical(hashed, jnp.int32(13))
    hashed = hashed * jnp.int32(-1028477387)
    hashed = hashed ^ lax.shift_right_logical(hashed, jnp.int32(16))
    return (hashed & 1023) >= 102


def kernel(
    seed_ref, grad_hbm, ctx_hbm, w_hbm, gc_hbm, gw_ref,
    grad, ctx, w, perm, g, wq, ctxe, acc, wt, own, cs, cr, zs, zr, total, yr, gcb,
    in_sem, out_sem, znews, ynews, gsend, grecv, csend, crecv, zsend, zrecv, ysend, yrecv,
):
    d = lax.axis_index("dp")
    t = lax.axis_index("tensor")
    core = lax.rem(d, 2)
    z = lax.rem(d // 2, NZ)
    yl = d // (2 * NZ)
    yh = t // NX
    x = lax.rem(t, NX)
    row = yh * NX
    other = (1 - yh) * NX
    xr, xl, xo = lax.rem(x + 1, NX), lax.rem(x + 3, NX), lax.rem(x + 2, NX)
    right, left, across = {"tensor": row + xr}, {"tensor": row + xl}, {"tensor": other + x}
    sibling = {"dp": d + 1 - 2 * core}
    owner = lax.rem(z, 2) == core

    def at(y_to, z_to, core_to):
        return {"dp": (y_to * NZ + z_to) * 2 + core_to}

    loads = [
        pltpu.make_async_copy(a, b, in_sem.at[i])
        for i, (a, b) in enumerate((
            (grad_hbm, grad),
            (w_hbm, w),
            (ctx_hbm, ctx.at[pl.ds(0, HQ)]),
            (ctx_hbm.at[pl.ds(256, 64)], ctx.at[pl.ds(HQ, 64)]),
        ))
    ]
    loads[0].start()

    barrier = pltpu.get_barrier_semaphore()

    def greet(device):
        pl.semaphore_signal(barrier, inc=1, device_id=device, device_id_type=MESH)

    def y_next(i):
        return at(lax.rem(yl + i + NY, NY), z, core)

    def z_next(i):
        return at(yl, lax.rem(z + i + NZ, NZ), core)

    greeted = (across, right, left, z_next(1), z_next(-1), y_next(1), y_next(-1), sibling)
    for device in greeted:
        greet(device)

    def tell(sem, devices):
        for device in devices:
            pl.semaphore_signal(sem, inc=1, device_id=device, device_id_type=MESH)

    def tell_near():
        tell(znews.at[0], (z_next(1), z_next(-1)))
        tell(ynews.at[0], (y_next(1), y_next(-1)))

    def tell_two():
        pl.semaphore_wait(znews.at[0], 2)
        tell(znews.at[1], (z_next(2), z_next(-2)))
        pl.semaphore_wait(ynews.at[0], 2)
        tell(ynews.at[1], (y_next(1), y_next(-1)))

    def tell_four():
        pl.semaphore_wait(znews.at[1], 2)
        tell(znews.at[2], (z_next(4), z_next(-4)))
        pl.semaphore_wait(ynews.at[1], 2)

    def all_in():
        pl.semaphore_wait(znews.at[2], 2)

    seed = seed_ref[0, 0]

    def feature_in_block(q, index):
        half, j = index // (PICK // 2), lax.rem(index // RUN, NZ // 2)
        return BLOCK * (2 * j + half) + RUN * q + lax.rem(index, RUN)

    def onehot(q):
        feature = feature_in_block(q, lax.broadcasted_iota(jnp.int32, (PICK, 1), 0))
        columns = lax.broadcasted_iota(jnp.int32, (PICK, BLOCK_Y), 1)
        perm[PICK * q:PICK * (q + 1)] = jnp.where(columns == feature, 1.0, 0.0).astype(jnp.bfloat16)

    def picked(a, p):
        return lax.dot_general(a, p, (((1,), (1,)), ((), ())), preferred_element_type=jnp.float32)

    first_position = (t * CHUNK + lax.broadcasted_iota(jnp.int32, (CHUNK, 1), 0)) * DW

    def prep_grad(parts):
        for y in range(NY):
            block = grad[:, BLOCK_Y * y:BLOCK_Y * (y + 1)]
            scaled = picked(block, perm[PICK * parts[0]:PICK * (parts[-1] + 1)]) * KEEP_SCALE
            for i, q in enumerate(parts):
                feature = feature_in_block(q, lax.broadcasted_iota(jnp.int32, (1, PICK), 1))
                keep = keep_bits(seed, first_position + (feature + y * BLOCK_Y))
                kept = jnp.where(keep, scaled[:, PICK * i:PICK * (i + 1)], 0.0)
                g[q, t, :, PICK * y:PICK * (y + 1)] = kept.astype(jnp.bfloat16)

    def prep_w():
        for y in range(NY):
            columns = picked(w[:, BLOCK_Y * y:BLOCK_Y * (y + 1)], perm[...]).astype(jnp.bfloat16)
            for q in range(PARTS):
                wq[q, :, PICK * y:PICK * (y + 1)] = columns[:, PICK * q:PICK * (q + 1)]

    whole, low, high = (0, 128), (0, 64), (64, 64)

    def piece(n, origin, rows):
        return g.at[n, origin, pl.ds(*rows)]

    def send(n, origin, rows, event, device):
        ref = piece(n, origin, rows)
        pltpu.make_async_remote_copy(
            src_ref=ref, dst_ref=ref, send_sem=gsend.at[n, event], recv_sem=grecv.at[n, event],
            device_id=device, device_id_type=MESH,
        ).start()

    def arrived(n, origin, rows, event):
        ref = piece(n, origin, rows)
        pltpu.make_async_copy(ref, ref, grecv.at[n, event]).wait()

    def sent(n, rows, event):
        ref = piece(n, t, rows)
        pltpu.make_async_copy(ref, ref, gsend.at[n, event]).wait()

    def send_own(n):
        send(n, t, whole, 0, right)
        send(n, t, whole, 1, left)

    def send_across(n):
        send(n, t, whole, 2, across)

    def relay_row(n):
        arrived(n, row + xl, whole, 0)
        send(n, row + xl, low, 3, right)
        arrived(n, row + xr, whole, 1)
        send(n, row + xr, high, 4, left)

    def relay_across(n):
        arrived(n, other + x, whole, 2)
        send(n, other + x, whole, 5, right)
        send(n, other + x, whole, 6, left)

    def relay_other(n):
        arrived(n, other + xl, whole, 5)
        send(n, other + xl, low, 7, right)
        arrived(n, other + xr, whole, 6)
        send(n, other + xr, high, 8, left)

    onehot(0)
    loads[0].wait()
    for load in loads[1:]:
        load.start()
    prep_grad((0,))
    pl.semaphore_wait(barrier, len(greeted))
    send_across(0)
    send_own(0)
    tell_near()
    for q in range(1, PARTS):
        onehot(q)
    prep_grad((1, 2))
    send_across(1)
    prep_grad((3, 4))
    sent(0, whole, 0)
    sent(0, whole, 1)
    send_own(1)
    relay_row(0)
    send_own(2)
    relay_across(0)

    def prepare():
        loads[1].wait()
        prep_w()
        loads[2].wait()
        loads[3].wait()
        for i in range(2 * NX):
            tokens = slice(i * CHUNK, (i + 1) * CHUNK)
            ctxe[tokens, :] = ctx[:, tokens].T
        acc[...] = jnp.zeros_like(acc)

    def rows_of(q, start):
        return g[q, pl.ds(start, NX)].reshape(NX * CHUNK, PART)

    def weight_term(q, start):
        tokens = pl.ds(pl.multiple_of(start * CHUNK, NX * CHUNK), NX * CHUNK)
        return lax.dot_general(
            rows_of(q, start), ctxe[tokens, :], (((0,), (0,)), ((), ())),
            preferred_element_type=jnp.float32,
        )

    def context_term(q, start):
        tokens = pl.ds(pl.multiple_of(start * CHUNK, NX * CHUNK), NX * CHUNK)
        acc[:, tokens] += picked(wq[q], rows_of(q, start))

    low_lanes = lax.broadcasted_iota(jnp.int32, (16, 128), 1) < 64

    def folded(half, j):
        runs = [
            pl.ds(pl.multiple_of(y * PICK + half * (PICK // 2) + j * RUN, RUN), RUN) for y in range(NY)
        ]
        last = [wt[run, 256:384] for run in runs]
        return (
            jnp.concatenate([wt[run, 0:128] for run in runs], axis=0),
            jnp.concatenate([wt[run, 128:256] for run in runs], axis=0),
            jnp.where(low_lanes, jnp.concatenate(last[:2], axis=0), jnp.concatenate(last[2:], axis=0)),
        )

    HALF = NZ // 4

    def pack(q):
        for h in range(2):
            for j in range(HALF * h, HALF * (h + 1)):
                a, b, c = folded(1 - core, j)
                cs[q, j, 0:32] = a.astype(jnp.bfloat16)
                cs[q, j, 32:64] = b.astype(jnp.bfloat16)
                cs[q, j, 64:80] = c.astype(jnp.bfloat16)
            to_sibling(q, h).start()
        for j in range(NZ // 2):
            own[j, 0:32], own[j, 32:64], own[j, 64:80] = folded(core, j)

    def to_sibling(q, h):
        half = pl.ds(HALF * h, HALF)
        return pltpu.make_async_remote_copy(
            src_ref=cs.at[q, half], dst_ref=cr.at[q, half],
            send_sem=csend.at[q, h], recv_sem=crecv.at[q, h],
            device_id=sibling, device_id_type=MESH,
        )

    def z_copy(q, j):
        return pltpu.make_async_remote_copy(
            src_ref=zs.at[q, j], dst_ref=zr.at[q, z], send_sem=zsend.at[q, j], recv_sem=zrecv.at[q],
            device_id=at(yl, 2 * j + core, core), device_id_type=MESH,
        )

    def z_stage(q):
        for h in range(2):
            to_sibling(q, h).wait_recv()
            for j in range(HALF * h, HALF * (h + 1)):
                zs[q, j] = (own[j] + cr[q, j].astype(jnp.float32)).astype(jnp.bfloat16)
            for i in (2, 1, 3, 0):
                j = HALF * h + lax.rem(z // 2 + i, HALF)

                @pl.when(2 * j + core != z)
                def _():
                    z_copy(q, j).start()

                @pl.when(2 * j + core == z)
                def _():
                    pltpu.make_async_copy(zs.at[q, j], zr.at[q, z], zrecv.at[q]).start()

    def y_copy(q, y_to, core_to, device):
        return pltpu.make_async_remote_copy(
            src_ref=total.at[q, y_to], dst_ref=yr.at[yl, q],
            send_sem=ysend.at[q, y_to, core_to], recv_sem=yrecv.at[yl, q],
            device_id=device, device_id_type=MESH,
        )

    def wanted(q, core_to):
        return q <= 2 if core_to == 0 else q >= 2

    def z_sum(q):
        @pl.when(owner)
        def _():
            pltpu.make_async_copy(zr.at[q], zr.at[q], zrecv.at[q]).wait()
            s = zr[q, 0].astype(jnp.float32)
            for i in range(1, NZ):
                s = s + zr[q, i].astype(jnp.float32)
            rolled = pltpu.roll(s[64:80], 64, 1)
            for y in range(NY):
                total[q, y, :, 0:128] = s[RUN * y:RUN * (y + 1)]
                total[q, y, :, 128:256] = s[32 + RUN * y:32 + RUN * (y + 1)]
                last = s[64:80] if y < 2 else rolled
                total[q, y, :, 256:384] = last[RUN * (y % 2):RUN * (y % 2 + 1)]
            yr[yl, q] = total[q, yl]
            for c in range(2):
                @pl.when(wanted(q, c))
                def _():
                    for i in (2, 1, 3):
                        y_to = lax.rem(yl + i, NY)
                        y_copy(q, y_to, c, at(y_to, z, c)).start()

                    @pl.when(core != c)
                    def _():
                        y_copy(q, yl, c, sibling).start()

    prepare()
    tell_two()

    def step(n, carry):
        relay_other(n)

        @pl.when(n == 0)
        def _():
            tell_four()

        arrived(n, row + xo, low, 3)
        arrived(n, row + xo, high, 4)
        wt[...] = weight_term(n, row)

        @pl.when(n + 1 < PARTS)
        def _():
            relay_row(n + 1)

        @pl.when(n + 2 < PARTS)
        def _():
            send_across(n + 2)

        @pl.when(n + 1 < PARTS)
        def _():
            relay_across(n + 1)

        context_term(n, row)
        arrived(n, other + xo, low, 7)
        arrived(n, other + xo, high, 8)
        wt[...] += weight_term(n, other)
        pack(n)
        context_term(n, other)

        @pl.when(n + 3 < PARTS)
        def _():
            send_own(n + 3)

        @pl.when(n == 0)
        def _():
            all_in()

        z_stage(n)

        @pl.when(n >= 2)
        def _():
            z_sum(n - 2)

        return carry

    lax.fori_loop(0, PARTS, step, 0)

    gcb[...] = acc[...].astype(jnp.bfloat16)
    store = pltpu.make_async_copy(gcb, gc_hbm, out_sem)
    store.start()

    z_sum(LAST - 1)

    def drain_z(q):
        block = zs.at[q, 0]
        for i in range(1, NZ // 2):
            pltpu.make_async_copy(block, block, zsend.at[q, lax.rem(z // 2 + i, NZ // 2)]).wait()

        @pl.when(jnp.logical_not(owner))
        def _():
            pltpu.make_async_copy(block, block, zsend.at[q, z // 2]).wait()

    def drain_y(q):
        for c in range(2):
            @pl.when(jnp.logical_and(owner, wanted(q, c)))
            def _():
                for y_to in range(NY):
                    @pl.when(jnp.logical_or(yl != y_to, core != c))
                    def _():
                        y_copy(q, y_to, c, sibling).wait_send()

    def drain(q, carry):
        for event in (2, 5, 6):
            sent(q, whole, event)
        for event in (3, 4, 7, 8):
            sent(q, low, event)

        @pl.when(q >= 1)
        def _():
            sent(q, whole, 0)
            sent(q, whole, 1)

        for h in range(2):
            to_sibling(q, h).wait_send()

        @pl.when(q < LAST)
        def _():
            drain_z(q)
            drain_y(q)

        return carry

    lax.fori_loop(0, PARTS, drain, 0)
    z_sum(LAST)
    drain_z(LAST)
    store.wait()

    def collect(q, carry):
        @pl.when(jnp.where(core == 0, q <= 2, q >= 2))
        def _():
            for s in range(NY):
                @pl.when(jnp.logical_or(jnp.logical_not(owner), yl != s))
                def _():
                    pltpu.make_async_copy(yr.at[s, q], yr.at[s, q], yrecv.at[s, q]).wait()

        return carry

    lax.fori_loop(0, PARTS, collect, 0)
    rows = []
    for i in range(3):
        q = 2 * core + i
        rows.append((yr[0, q] + yr[1, q]) + (yr[2, q] + yr[3, q]))
    done = jnp.concatenate(rows, axis=0)
    gw_ref[...] = jnp.where(core == 0, done[0:20], done[4:24])[:, 0:HQ]

    drain_y(LAST)


def hand_over(a_ref, b_ref, a_out, b_out):
    a_out[...] = a_ref[...]
    b_out[...] = b_ref[...]


def shards(out_grad, context, out_weight, dropout_seeds):
    bf16, f32 = jnp.bfloat16, jnp.float32
    dma = pltpu.SemaphoreType.DMA
    hbm = pl.BlockSpec(memory_space=pltpu.HBM)
    tokens = 2 * NX * CHUNK
    grad_ctx, weight_grad = pl.pallas_call(
        kernel,
        out_shape=(
            jax.ShapeDtypeStruct((HQ, tokens), bf16),
            jax.ShapeDtypeStruct((20, HQ), f32),
        ),
        in_specs=[pl.BlockSpec(memory_space=pltpu.SMEM), hbm, hbm, hbm],
        out_specs=(hbm, pl.BlockSpec(memory_space=pltpu.VMEM)),
        scratch_shapes=[
            pltpu.VMEM((CHUNK, DW), bf16),
            pltpu.VMEM((LANES, tokens), bf16),
            pltpu.VMEM((HQ, DW), bf16),
            pltpu.VMEM((BLOCK_Y, BLOCK_Y), bf16),
            pltpu.VMEM((PARTS, 2 * NX, CHUNK, PART), bf16),
            pltpu.VMEM((PARTS, HQ, PART), bf16),
            pltpu.VMEM((tokens, LANES), bf16),
            pltpu.VMEM((HQ, tokens), f32),
            pltpu.VMEM((PART, LANES), f32),
            pltpu.VMEM((NZ // 2, FOLD, 128), f32),
            pltpu.VMEM((PARTS, NZ // 2, FOLD, 128), bf16),
            pltpu.VMEM((PARTS, NZ // 2, FOLD, 128), bf16),
            pltpu.VMEM((PARTS, NZ // 2, FOLD, 128), bf16),
            pltpu.VMEM((PARTS, NZ, FOLD, 128), bf16),
            pltpu.VMEM((PARTS, NY, RUN, LANES), f32),
            pltpu.VMEM((NY, PARTS, RUN, LANES), f32),
            pltpu.VMEM((HQ, tokens), bf16),
            dma((4,)),
            dma,
            pltpu.SemaphoreType.REGULAR((3,)),
            pltpu.SemaphoreType.REGULAR((2,)),
            dma((PARTS, 9)),
            dma((PARTS, 9)),
            dma((PARTS, 2)),
            dma((PARTS, 2)),
            dma((PARTS, NZ // 2)),
            dma((PARTS,)),
            dma((PARTS, NY, 2)),
            dma((NY, PARTS)),
        ],
        compiler_params=pltpu.CompilerParams(
            collective_id=0, has_side_effects=True, vmem_limit_bytes=56 * 2**20
        ),
        cost_estimate=pl.CostEstimate(flops=4 * tokens * DW * HQ, bytes_accessed=4 << 20, transcendentals=0),
    )(dropout_seeds, out_grad, context.T, out_weight.T)
    grad_ctx, weight_grad = pl.pallas_call(
        hand_over,
        out_shape=(
            jax.ShapeDtypeStruct((HQ, tokens), bf16),
            jax.ShapeDtypeStruct((20, HQ), f32),
        ),
        in_specs=[pl.BlockSpec(memory_space=pltpu.VMEM)] * 2,
        out_specs=[pl.BlockSpec(memory_space=pltpu.VMEM)] * 2,
        cost_estimate=pl.CostEstimate(flops=0, bytes_accessed=2 << 20, transcendentals=0),
    )(grad_ctx, weight_grad)
    return grad_ctx.T, weight_grad


def solution(mesh):
    placed = (P(("dp", "tensor"), None), P("dp", "tensor"), P(None, "tensor"), P("dp", None))
    return jax.shard_map(
        shards,
        mesh=mesh,
        in_specs=placed,
        out_specs=(P("dp", "tensor"), P("dp", "tensor")),
        check_vma=False,
    )
```
